256 devices in a mesh: tm: 32 (over z, x_lo, core), tile: 8 (over y, x_hi).
Axes of the slice: x: 4 (x_hi: 2, x_lo: 2; x = x_hi * 2 + x_lo), y: 4, z: 8, core: 2. Of those that a mesh axis runs over, the one named last changes fastest.
Arguments:
- queries: bfloat16 [256, 192, 3072], P(('tm', 'tile')), may hold values from -120 to 120
- keys: bfloat16 [256, 192, 3072], P(('tm', 'tile')), may hold values from -4.6 to 4.6
- values: bfloat16 [256, 192, 3072], P(('tm', 'tile')), may hold values from -6 to 6
- grad_out: bfloat16 [256, 192, 3072], P(('tm', 'tile')), may hold values from -6 to 6
Outputs:
- grad_queries: bfloat16 [256, 192, 3072], P('tm', 'tile')
- grad_keys: bfloat16 [256, 192, 3072], P('tm', 'tile')
- grad_values: bfloat16 [256, 192, 3072], P('tm', 'tile')
The draws below stay inside these ranges and needn't reach their ends.
All inputs are finite; a program needn't handle non-finite values.
Results may differ from the reference program's by a relative error of at most 0.011.
Values may be sent and summed in bfloat16 or wider, within the bound.
No kernel may reach another device: no remote copies, remote signals or barrier semaphores. Data moves between devices by JAX's collectives and lax.ppermute only.
A program may use at most 128 MiB of HBM per device.

```python
import math
import jax
import jax.numpy as jnp
from jax import lax

H = 24
DH = 128
FR_DEV = 8
SP_DEV = 24
FRAMES = 256
SPATIAL = 192
N_TM = 32
N_TILE = 8


def paired_keys(key, spread):
    first = jax.random.normal(jax.random.fold_in(key, 101), (FRAMES, SPATIAL, H * DH), jnp.float32)
    second = jax.random.normal(jax.random.fold_in(key, 102), (FRAMES, SPATIAL, H * DH), jnp.float32)
    shifted = jnp.roll(first, 1, axis=1)
    odd_rows = (jnp.arange(SPATIAL) % 2 == 1)[None, :, None]
    mixed = (shifted + spread * second) / jnp.sqrt(1.0 + spread * spread)
    return jnp.clip(jnp.where(odd_rows, mixed, first), -4.6, 4.6)


def draw_keys(key, part):
    spread = 3.0
    return paired_keys(key, spread).astype(jnp.bfloat16)


def draw_queries(key, part):
    own_key = jax.random.fold_in(key, 7)
    result = jnp.clip(jax.random.normal(own_key, (FRAMES, SPATIAL, H * DH), jnp.float32), -6.0, 6.0)
    return result.astype(jnp.bfloat16)


def levels(stream_key, extent, shards, least, largest):
    gain = 1.0
    for dim, parts in shards:
        steps = jax.random.uniform(jax.random.fold_in(jax.random.fold_in(stream_key, 6), dim), (parts,), jnp.float32, least / len(shards), largest / len(shards))
        gain = gain * jnp.repeat(jnp.exp(steps), extent[dim] // parts).reshape((-1,) + (1,) * (len(extent) - 1 - dim))
    return gain


def normal_values(key, shape, scale, most, pieces=(), kind=jnp.bfloat16):
    array = jax.random.normal(key, shape, jnp.float32) * scale
    if len(pieces) > 0:
        array = levels(key, shape, pieces, -0.22, 0.18) * array
    return jnp.clip(array, min=-most, max=most).astype(kind)


def setup_inputs(seed: int = 0) -> dict:
    seeds = jax.random.split(jax.random.key(seed), 5)
    queries = draw_queries(jax.random.fold_in(seeds[4], 71), 0)
    keys = draw_keys(jax.random.fold_in(seeds[4], 71), 0)
    values = normal_values(seeds[2], (FRAMES, SPATIAL, H * DH), 1.0, 6.0, ((0, 256),))
    grad_out = normal_values(seeds[3], (FRAMES, SPATIAL, H * DH), 1.0, 6.0, ((0, 256),))
    return dict(queries=queries, keys=keys, values=values, grad_out=grad_out)


def to_blocks(source):
    shaped = source.reshape(N_TM, FR_DEV, N_TILE, SP_DEV, H, DH)
    return shaped.transpose(0, 2, 1, 3, 4, 5).reshape(N_TM, N_TILE, FR_DEV * SP_DEV, H, DH)

def from_blocks(block):
    shaped = block.reshape(N_TM, N_TILE, FR_DEV, SP_DEV, H * DH)
    return shaped.transpose(0, 2, 1, 3, 4).reshape(FRAMES, SPATIAL, H * DH)

def window(block, first_slab):
    slab_list = ((first_slab + jnp.arange(4, dtype=jnp.int32)) % N_TM).astype(jnp.int32)
    picked = jnp.take(block, slab_list, axis=0)
    return picked.transpose(1, 0, 2, 3, 4).reshape(N_TILE, 4 * FR_DEV * SP_DEV, H, DH).astype(jnp.float32)

def window_stat(stat, first_slab):
    slab_list = ((first_slab + jnp.arange(4, dtype=jnp.int32)) % N_TM).astype(jnp.int32)
    picked = jnp.take(stat, slab_list, axis=0)
    return picked.transpose(1, 2, 0, 3).reshape(N_TILE, H, 4 * FR_DEV * SP_DEV)

def rounded(source):
    return lax.optimization_barrier(source.astype(jnp.bfloat16)).astype(jnp.float32)

def reference(queries, keys, values, grad_out):
    scaling = 1.0 / math.sqrt(DH)
    query_blocks = to_blocks(queries)
    key_blocks = to_blocks(keys)
    value_blocks = to_blocks(values)
    grad_blocks = to_blocks(grad_out)

    def stats(slab_index):
        query_here = query_blocks[slab_index].astype(jnp.float32)
        grad_here = grad_blocks[slab_index].astype(jnp.float32)
        key_window = window(key_blocks, slab_index - 3)
        value_window = window(value_blocks, slab_index - 3)
        scores = jnp.einsum('trhd,tkhd->thrk', query_here, key_window) * scaling
        peak = lax.optimization_barrier(jnp.max(scores, axis=-1, keepdims=True))
        log_total = peak[..., 0] + jnp.log(lax.optimization_barrier(jnp.sum(jnp.exp(scores - peak), axis=-1)))
        weights = rounded(jnp.exp(scores - log_total[..., None]))
        output = jnp.einsum('thrk,tkhd->trhd', weights, value_window)
        row_delta = lax.optimization_barrier(jnp.sum(grad_here * output, axis=-1)).transpose(0, 2, 1)
        return (log_total, row_delta)
    log_totals, deltas = lax.map(stats, jnp.arange(N_TM, dtype=jnp.int32))

    def grads(slab_index):
        query_here = query_blocks[slab_index].astype(jnp.float32)
        grad_here = grad_blocks[slab_index].astype(jnp.float32)
        key_window = window(key_blocks, slab_index - 3)
        value_window = window(value_blocks, slab_index - 3)
        scores = jnp.einsum('trhd,tkhd->thrk', query_here, key_window) * scaling
        weights = jnp.exp(scores - log_totals[slab_index][..., None])
        dprobs = jnp.einsum('trhd,tkhd->thrk', grad_here, value_window)
        dscores = rounded(weights * (dprobs - deltas[slab_index][..., None]))
        grad_query = (jnp.einsum('thrk,tkhd->trhd', dscores, key_window) * scaling).astype(jnp.bfloat16)
        query_window = window(query_blocks, slab_index)
        grad_window = window(grad_blocks, slab_index)
        total_window = window_stat(log_totals, slab_index)
        delta_window = window_stat(deltas, slab_index)
        key_here = key_blocks[slab_index].astype(jnp.float32)
        value_here = value_blocks[slab_index].astype(jnp.float32)
        back_scores = jnp.einsum('tqhd,tkhd->thqk', query_window, key_here) * scaling
        back_weights = jnp.exp(back_scores - total_window[..., None])
        back_dprobs = jnp.einsum('tqhd,tkhd->thqk', grad_window, value_here)
        back_dscores = rounded(back_weights * (back_dprobs - delta_window[..., None]))
        grad_key = (jnp.einsum('thqk,tqhd->tkhd', back_dscores, query_window) * scaling).astype(jnp.bfloat16)
        grad_value = jnp.einsum('thqk,tqhd->tkhd', rounded(back_weights), grad_window).astype(jnp.bfloat16)
        return (grad_query, grad_key, grad_value)
    grad_query_blocks, grad_key_blocks, grad_value_blocks = lax.map(grads, jnp.arange(N_TM, dtype=jnp.int32))
    return (from_blocks(grad_query_blocks), from_blocks(grad_key_blocks), from_blocks(grad_value_blocks))
```

```python
import math

import jax
import jax.numpy as jnp
from jax import lax
from jax.experimental import pallas as pl
from jax.experimental.pallas import tpu as pltpu
from jax.sharding import Mesh, PartitionSpec as P

DH = 128
HEADS = 24
FRAMES = 8
SPOTS = 24
GROUP = 4
PLANES = 8
ROWS = FRAMES * SPOTS
OWN = GROUP * ROWS
HALO = 3 * ROWS
MINE = HEADS // GROUP
CHUNKS = (3, 3)
SCALE = 1.0 / math.sqrt(DH)
SCALE2 = SCALE * math.log2(math.e)
BF16 = jnp.bfloat16
F32 = jnp.float32
ANY = pl.BlockSpec(memory_space=pl.ANY)


def nt(a, b):
    return lax.dot_general(a, b, (((1,), (1,)), ((), ())), preferred_element_type=F32)


def nn(a, b):
    return lax.dot_general(a, b, (((1,), (0,)), ((), ())), preferred_element_type=F32)


def tn(a, b):
    return lax.dot_general(a, b, (((0,), (0,)), ((), ())), preferred_element_type=F32)


def pack_kernel(first, heads, *refs):
    sources, (packed, sems) = refs[:4], refs[4:]
    width = heads * DH
    copies = []
    for group in range(GROUP):
        for index, source in enumerate(sources):
            start = (group * MINE + first) * DH
            copies.append(
                pltpu.make_async_copy(
                    source.at[:, :, pl.ds(start, width)],
                    packed.at[group, :, :, pl.ds(index * width, width)],
                    sems.at[group * 4 + index],
                )
            )
    for copy in copies:
        copy.start()
    for copy in copies:
        copy.wait()


def pack(sources, first, heads):
    def body(*refs):
        pack_kernel(first, heads, *refs)

    return pl.pallas_call(
        body,
        out_shape=jax.ShapeDtypeStruct((GROUP, FRAMES, SPOTS, 4 * heads * DH), BF16),
        in_specs=[ANY] * 4,
        out_specs=ANY,
        scratch_shapes=[pltpu.SemaphoreType.DMA((16,))],
        name="pack",
    )(*sources)


def own_kernel(q, k, v, g, hk, hv, dq, dk, dv, stats, kx, vx):
    kx[:HALO] = hk[...]
    kx[HALO:] = k[...]
    vx[:HALO] = hv[...]
    vx[HALO:] = v[...]
    for slab in range(GROUP):
        here = slice(slab * ROWS, (slab + 1) * ROWS)
        seen = slice(slab * ROWS, (slab + 4) * ROWS)
        qs, gs = q[here], g[here]
        ks, vs = kx[seen], vx[seen]
        scores = nt(ks, qs)
        peak = jnp.max(scores, axis=0, keepdims=True) * SCALE2
        weights = jnp.exp2(scores * SCALE2 - peak)
        total = jnp.sum(weights, axis=0, keepdims=True)
        probs = weights * (1.0 / total)
        dprobs = nt(vs, gs)
        delta = jnp.sum(probs * dprobs, axis=0, keepdims=True)
        dscores = (probs * (dprobs - delta)).astype(BF16)
        low = probs.astype(BF16)
        stats[0, 2 * slab : 2 * slab + 1] = peak + jnp.log2(total)
        stats[0, 2 * slab + 1 : 2 * slab + 2] = delta
        dq[here] = (tn(dscores, ks) * SCALE).astype(BF16)
        part_k = nn(dscores[(3 - slab) * ROWS :], qs)
        part_v = nn(low[(3 - slab) * ROWS :], gs)
        if slab:
            dk[: slab * ROWS] += part_k[: slab * ROWS]
            dv[: slab * ROWS] += part_v[: slab * ROWS]
        dk[here] = part_k[slab * ROWS :]
        dv[here] = part_v[slab * ROWS :]


def own_pass(rows, halo, heads):
    def col(index):
        return pl.BlockSpec((OWN, DH), lambda h: (0, index * heads + h))

    def halo_col(index):
        return pl.BlockSpec((HALO, DH), lambda h: (0, index * heads + h))

    out = pl.BlockSpec((OWN, DH), lambda h: (0, h))
    return pl.pallas_call(
        own_kernel,
        grid=(heads,),
        in_specs=[col(2), col(0), col(1), col(3), halo_col(0), halo_col(1)],
        out_specs=[out, out, out, pl.BlockSpec((1, 8, ROWS), lambda h: (h, 0, 0))],
        out_shape=[
            jax.ShapeDtypeStruct((OWN, heads * DH), BF16),
            jax.ShapeDtypeStruct((OWN, heads * DH), F32),
            jax.ShapeDtypeStruct((OWN, heads * DH), F32),
            jax.ShapeDtypeStruct((heads, 8, ROWS), F32),
        ],
        scratch_shapes=[pltpu.VMEM((OWN + HALO, DH), BF16)] * 2,
        compiler_params=pltpu.CompilerParams(vmem_limit_bytes=40 << 20),
        cost_estimate=pl.CostEstimate(
            flops=heads * 16 * 2 * 5 * ROWS * ROWS * DH * 4,
            bytes_accessed=heads * OWN * DH * 24,
            transcendentals=heads * 16 * ROWS * ROWS,
        ),
        name="own_pass",
    )(rows, rows, rows, rows, halo, halo)


def later_kernel(k, v, hq, hg, stats, dk, dv, out, sk, sv):
    sk[...] = dk[...]
    sv[...] = dv[...]
    for slab in range(3):
        there = slice(slab * ROWS, (slab + 1) * ROWS)
        rest = slice((slab + 1) * ROWS, OWN)
        qs, gs = hq[there], hg[there]
        lse = stats[0, 2 * slab : 2 * slab + 1]
        delta = stats[0, 2 * slab + 1 : 2 * slab + 2]
        probs = jnp.exp2(nt(k[rest], qs) * SCALE2 - lse)
        dscores = (probs * (nt(v[rest], gs) - delta)).astype(BF16)
        sk[rest] += nn(dscores, qs)
        sv[rest] += nn(probs.astype(BF16), gs)
    for slab in range(GROUP):
        here = slice(slab * ROWS, (slab + 1) * ROWS)
        out[slab, 0] = (sk[here] * SCALE).astype(BF16)
        out[slab, 1] = sv[here].astype(BF16)


def later_pass(rows, halo, stats, dk, dv, heads):
    def col(index):
        return pl.BlockSpec((OWN, DH), lambda h: (0, index * heads + h))

    def halo_col(index):
        return pl.BlockSpec((HALO, DH), lambda h: (0, index * heads + h))

    return pl.pallas_call(
        later_kernel,
        grid=(heads,),
        in_specs=[
            col(0),
            col(1),
            halo_col(0),
            halo_col(1),
            pl.BlockSpec((1, 8, ROWS), lambda h: (h, 0, 0)),
            col(0),
            col(0),
        ],
        out_specs=pl.BlockSpec((GROUP, 2, ROWS, DH), lambda h: (0, 0, 0, h)),
        out_shape=jax.ShapeDtypeStruct((GROUP, 2, ROWS, heads * DH), BF16),
        scratch_shapes=[pltpu.VMEM((OWN, DH), F32)] * 2,
        compiler_params=pltpu.CompilerParams(vmem_limit_bytes=40 << 20),
        cost_estimate=pl.CostEstimate(
            flops=heads * 6 * 2 * 4 * ROWS * ROWS * DH * 4,
            bytes_accessed=heads * OWN * DH * 20,
            transcendentals=heads * 6 * ROWS * ROWS,
        ),
        name="later_pass",
    )(rows, rows, halo, halo, stats, dk, dv)


def unpack_kernel(*refs):
    count = len(CHUNKS)
    pieces_q, pieces_kv = refs[:count], refs[count : 2 * count]
    out_q, out_k, out_v, sems = refs[2 * count :]
    copies = []
    first = 0
    for chunk, heads in enumerate(CHUNKS):
        for group in range(GROUP):
            place = pl.ds((group * MINE + first) * DH, heads * DH)
            for source, target in (
                (pieces_q[chunk].at[group], out_q),
                (pieces_kv[chunk].at[group, 0], out_k),
                (pieces_kv[chunk].at[group, 1], out_v),
            ):
                copies.append(
                    pltpu.make_async_copy(source, target.at[:, place], sems.at[len(copies)])
                )
        first += heads
    for copy in copies:
        copy.start()
    for copy in copies:
        copy.wait()


def unpack(pieces_q, pieces_kv):
    shape = jax.ShapeDtypeStruct((ROWS, HEADS * DH), BF16)
    return pl.pallas_call(
        unpack_kernel,
        out_shape=[shape] * 3,
        in_specs=[ANY] * (2 * len(CHUNKS)),
        out_specs=[ANY] * 3,
        scratch_shapes=[pltpu.SemaphoreType.DMA((len(CHUNKS) * GROUP * 3,))],
        name="unpack",
    )(*pieces_q, *pieces_kv)


def to_plane(block, step):
    return lax.ppermute(block, "z", [(i, (i + step) % PLANES) for i in range(PLANES)])


def shards(queries, keys, values, grad_out):
    sources = [a.reshape(FRAMES, SPOTS, HEADS * DH) for a in (keys, values, queries, grad_out)]
    pieces_q, pieces_kv = [], []
    first = 0
    for heads in CHUNKS:
        width = heads * DH
        packed = pack(sources, first, heads).reshape(GROUP * FRAMES, SPOTS, 4 * width)
        got = lax.all_to_all(packed, ("g", "tile"), 0, 0, tiled=True)
        rows = got.reshape(OWN, 4 * width)
        earlier = to_plane(rows[ROWS:, : 2 * width], 1)
        later = to_plane(rows[:HALO, 2 * width :], -1)
        dq, dk, dv, stats = own_pass(rows, earlier, heads)
        later_stats = to_plane(stats, -1)
        dkv = later_pass(rows, later, later_stats, dk, dv, heads)
        pieces_q.append(lax.all_to_all(dq.reshape(GROUP, ROWS, width), "g", 0, 0, tiled=True))
        pieces_kv.append(lax.all_to_all(dkv, "g", 0, 0, tiled=True))
        first += heads
    outs = unpack(pieces_q, pieces_kv)
    return tuple(out.reshape(FRAMES, SPOTS, HEADS * DH) for out in outs)


def solution(mesh):
    parted = Mesh(mesh.devices.reshape(PLANES, GROUP, FRAMES), ("z", "g", "tile"))
    given = P(("z", "g", "tile"), None, None)
    wanted = P(("z", "g"), "tile", None)
    return jax.shard_map(
        shards, mesh=parted, in_specs=(given,) * 4, out_specs=(wanted,) * 3, check_vma=False
    )
```

```python
import math

import jax
import jax.numpy as jnp
from jax import lax
from jax.experimental import pallas as pl
from jax.experimental.pallas import tpu as pltpu
from jax.sharding import Mesh, PartitionSpec as P

DH = 128
HEADS = 24
FRAMES = 8
SPOTS = 24
GROUP = 4
PLANES = 8
ROWS = FRAMES * SPOTS
OWN = GROUP * ROWS
HALO = 3 * ROWS
MINE = HEADS // GROUP
CHUNKS = (3, 3)
SCALE = 1.0 / math.sqrt(DH)
SCALE2 = SCALE * math.log2(math.e)
BF16 = jnp.bfloat16
F32 = jnp.float32
ANY = pl.BlockSpec(memory_space=pl.ANY)
PLACE = pl.BlockSpec(memory_space=pltpu.SMEM)


def nt(a, b):
    return lax.dot_general(a, b, (((1,), (1,)), ((), ())), preferred_element_type=F32)


def nn(a, b):
    return lax.dot_general(a, b, (((1,), (0,)), ((), ())), preferred_element_type=F32)


def tn(a, b):
    return lax.dot_general(a, b, (((0,), (0,)), ((), ())), preferred_element_type=F32)


def pack_kernel(parts, *refs):
    sources, (packed, held, sems) = refs[: len(parts)], refs[len(parts) :]
    loads, stores = [], []
    column = 0
    for index, (source, (_, first, heads)) in enumerate(zip(sources, parts)):
        width = heads * DH
        for group in range(GROUP):
            place = index * GROUP + group
            start = (group * MINE + first) * DH
            slot = held.at[place, :, :, pl.ds(0, width)]
            loads.append(
                pltpu.make_async_copy(
                    source.at[:, :, pl.ds(start, width)], slot, sems.at[0, place]
                )
            )
            stores.append(
                pltpu.make_async_copy(
                    slot, packed.at[group, :, :, pl.ds(column, width)], sems.at[1, place]
                )
            )
        column += width
    for load in loads:
        load.start()
    for load, store in zip(loads, stores):
        load.wait()
        store.start()
    for store in stores:
        store.wait()


def pack(tensors, parts):
    def body(*refs):
        pack_kernel(parts, *refs)

    count = len(parts) * GROUP
    most = max(heads for _, _, heads in parts)
    total = sum(heads for _, _, heads in parts)
    packed = pl.pallas_call(
        body,
        out_shape=jax.ShapeDtypeStruct((GROUP, FRAMES, SPOTS, total * DH), BF16),
        in_specs=[ANY] * len(parts),
        out_specs=ANY,
        scratch_shapes=[
            pltpu.VMEM((count, FRAMES, SPOTS, most * DH), BF16),
            pltpu.SemaphoreType.DMA((2, count)),
        ],
        compiler_params=pltpu.CompilerParams(vmem_limit_bytes=60 << 20),
        name="pack",
    )(*[tensors[name] for name, _, _ in parts])
    return packed.reshape(GROUP * FRAMES, SPOTS, total * DH)


def partner_of(place, partner):
    return lax.bitwise_xor(place, jnp.int32(partner))


def partner_rows(place, partner):
    return pl.ds(pl.multiple_of(partner_of(place[0], partner) * ROWS, ROWS), ROWS)


def slab_rows(first, count=1):
    return slice(first * ROWS, (first + count) * ROWS)


def own_kernel(place, q, k, v, g, hk, hv, *refs):
    (dk, dv, stats), dq_to, (dq, kx, vx) = refs[:3], refs[3:7], refs[7:]
    kx[:HALO] = hk[...]
    kx[HALO:] = k[...]
    vx[:HALO] = hv[...]
    vx[HALO:] = v[...]
    fronts = []
    for slab in range(GROUP):
        here, seen = slab_rows(slab), slab_rows(slab, 4)
        fronts.append((nt(kx[seen], q[here]), nt(vx[seen], g[here])))
    for slab, (scores, dprobs) in enumerate(fronts):
        here, seen, past = slab_rows(slab), slab_rows(slab, 4), slab * ROWS
        peak = jnp.max(scores, axis=0, keepdims=True) * SCALE2
        weights = jnp.exp2(scores * SCALE2 - peak)
        total = jnp.sum(weights, axis=0, keepdims=True)
        probs = weights * (1.0 / total)
        delta = jnp.sum(probs * dprobs, axis=0, keepdims=True)
        dscores = (probs * (dprobs - delta)).astype(BF16)
        low = probs.astype(BF16)
        stats[0, 2 * slab : 2 * slab + 1] = peak + jnp.log2(total)
        stats[0, 2 * slab + 1 : 2 * slab + 2] = delta
        dq[here] = (tn(kx[seen], dscores).T * SCALE).astype(BF16)
        part_k = nn(dscores[HALO - past :], q[here])
        part_v = nn(low[HALO - past :], g[here])
        if slab:
            dk[0, :past] += part_k[:past]
            dv[0, :past] += part_v[:past]
        dk[0, here] = part_k[past:]
        dv[0, here] = part_v[past:]
    for partner, target in enumerate(dq_to):
        target[...] = dq[partner_rows(place, partner)]


def own_pass(place, rows, halo, heads, room):
    def col(start, rows=OWN):
        return pl.BlockSpec((rows, DH), lambda h: (0, start + h))

    part = pl.BlockSpec((1, OWN, DH), lambda h: (h, 0, 0))
    return pl.pallas_call(
        own_kernel,
        grid=(heads,),
        in_specs=[
            PLACE,
            col(2 * heads),
            col(0),
            col(heads),
            col(3 * heads),
            col(0, HALO),
            col(heads, HALO),
        ],
        out_specs=[part, part, pl.BlockSpec((1, 8, ROWS), lambda h: (h, 0, 0))]
        + [col(0, ROWS)] * GROUP,
        out_shape=[
            jax.ShapeDtypeStruct((heads, OWN, DH), F32),
            jax.ShapeDtypeStruct((heads, OWN, DH), F32),
            jax.ShapeDtypeStruct((heads, 8, ROWS), F32),
        ]
        + [jax.ShapeDtypeStruct((ROWS, heads * DH), BF16)] * GROUP,
        scratch_shapes=[pltpu.VMEM((OWN, DH), BF16)]
        + [pltpu.VMEM((OWN + HALO, DH), BF16)] * 2,
        compiler_params=pltpu.CompilerParams(vmem_limit_bytes=room << 20),
        cost_estimate=pl.CostEstimate(
            flops=1000,
            bytes_accessed=1000,
            transcendentals=0,
        ),
        name="own_pass",
    )(place, rows, rows, rows, rows, halo, halo)


def later_kernel(place, k, v, hq, hg, stats, dk, dv, *refs):
    outs, (sk, sv) = refs[:GROUP], refs[GROUP:]
    sk[...] = dk[0]
    sv[...] = dv[0]
    fronts = []
    for slab in range(3):
        there, rest = slab_rows(slab), slice((slab + 1) * ROWS, OWN)
        fronts.append((nt(k[rest], hq[there]), nt(v[rest], hg[there])))
    for slab, (scores, dprobs) in enumerate(fronts):
        there, rest = slab_rows(slab), slice((slab + 1) * ROWS, OWN)
        lse = stats[0, 2 * slab : 2 * slab + 1]
        delta = stats[0, 2 * slab + 1 : 2 * slab + 2]
        probs = jnp.exp2(scores * SCALE2 - lse)
        dscores = (probs * (dprobs - delta)).astype(BF16)
        sk[rest] += nn(dscores, hq[there])
        sv[rest] += nn(probs.astype(BF16), hg[there])
    for partner, target in enumerate(outs):
        here = partner_rows(place, partner)
        target[0] = (sk[here] * SCALE).astype(BF16)
        target[1] = sv[here].astype(BF16)


def later_pass(place, rows, halo, stats, dk, dv, heads, room):
    def col(start, rows=OWN):
        return pl.BlockSpec((rows, DH), lambda h: (0, start + h))

    part = pl.BlockSpec((1, OWN, DH), lambda h: (h, 0, 0))
    return pl.pallas_call(
        later_kernel,
        grid=(heads,),
        in_specs=[
            PLACE,
            col(0),
            col(heads),
            col(0, HALO),
            col(heads, HALO),
            pl.BlockSpec((1, 8, ROWS), lambda h: (h, 0, 0)),
            part,
            part,
        ],
        out_specs=[pl.BlockSpec((2, ROWS, DH), lambda h: (0, 0, h))] * GROUP,
        out_shape=[jax.ShapeDtypeStruct((2, ROWS, heads * DH), BF16)] * GROUP,
        scratch_shapes=[pltpu.VMEM((OWN, DH), F32)] * 2,
        compiler_params=pltpu.CompilerParams(vmem_limit_bytes=room << 20),
        cost_estimate=pl.CostEstimate(
            flops=1000,
            bytes_accessed=1000,
            transcendentals=0,
        ),
        name="later_pass",
    )(place, rows, rows, halo, halo, stats, dk, dv)


def unpack_kernel(place, *refs):
    count = 2 * len(CHUNKS) * GROUP
    pieces, outs, (held, load_sems, store_sems) = refs[:count], refs[count : count + 3], refs[count + 3 :]
    loads = [[], [], []]
    first = 0
    for chunk, heads in enumerate(CHUNKS):
        for partner in range(GROUP):
            column = (partner_of(place[0], partner) * MINE + first) * DH
            columns = pl.ds(pl.multiple_of(column, DH), heads * DH)
            dq = pieces[2 * chunk * GROUP + partner]
            dkv = pieces[(2 * chunk + 1) * GROUP + partner]
            for index, source in enumerate((dq, dkv.at[0], dkv.at[1])):
                loads[index].append(
                    pltpu.make_async_copy(
                        source,
                        held.at[index, :, columns],
                        load_sems.at[index, chunk * GROUP + partner],
                    )
                )
        first += heads
    for load in loads[0] + loads[1] + loads[2]:
        load.start()
    stores = []
    for index in range(3):
        for load in loads[index]:
            load.wait()
        stores.append(pltpu.make_async_copy(held.at[index], outs[index], store_sems.at[index]))
        stores[-1].start()
    for store in stores:
        store.wait()


def unpack(place, pieces):
    shape = jax.ShapeDtypeStruct((ROWS, HEADS * DH), BF16)
    return pl.pallas_call(
        unpack_kernel,
        out_shape=[shape] * 3,
        in_specs=[PLACE] + [ANY] * len(pieces),
        out_specs=[ANY] * 3,
        scratch_shapes=[
            pltpu.VMEM((3, ROWS, HEADS * DH), BF16),
            pltpu.SemaphoreType.DMA((3, len(CHUNKS) * GROUP)),
            pltpu.SemaphoreType.DMA((3,)),
        ],
        compiler_params=pltpu.CompilerParams(vmem_limit_bytes=8 << 20),
        name="unpack",
    )(place, *pieces)


def edges_kernel(rows, kv, qg, held_kv, held_qg, sems):
    width = kv.shape[1]
    loads = (
        pltpu.make_async_copy(rows.at[pl.ds(ROWS, HALO), pl.ds(0, width)], held_kv, sems.at[0]),
        pltpu.make_async_copy(rows.at[pl.ds(0, HALO), pl.ds(width, width)], held_qg, sems.at[1]),
    )
    stores = (
        pltpu.make_async_copy(held_kv, kv, sems.at[2]),
        pltpu.make_async_copy(held_qg, qg, sems.at[3]),
    )
    for load in loads:
        load.start()
    for load, store in zip(loads, stores):
        load.wait()
        store.start()
    for store in stores:
        store.wait()


def edges(rows):
    width = rows.shape[1] // 2
    return pl.pallas_call(
        edges_kernel,
        out_shape=[jax.ShapeDtypeStruct((HALO, width), BF16)] * 2,
        in_specs=[ANY],
        out_specs=[ANY] * 2,
        scratch_shapes=[pltpu.VMEM((HALO, width), BF16)] * 2 + [pltpu.SemaphoreType.DMA((4,))],
        compiler_params=pltpu.CompilerParams(vmem_limit_bytes=60 << 20),
        name="edges",
    )(rows)


def to_plane(block, step):
    return lax.ppermute(block, "z", [(i, (i + step) % PLANES) for i in range(PLANES)])


def to_tiles(tensors, parts):
    got = lax.all_to_all(pack(tensors, parts), ("g", "tile"), 0, 0, tiled=True)
    return got.reshape(OWN, -1)


def to_slabs(blocks):
    sent = [
        lax.ppermute(block, "g", [(i, i ^ partner) for i in range(GROUP)])
        for partner, block in enumerate(blocks)
        if partner
    ]
    return [blocks[0], *sent]


def tied(*arrays):
    return lax.optimization_barrier(arrays)


def shards(queries, keys, values, grad_out):
    tensors = {
        name: a.reshape(FRAMES, SPOTS, HEADS * DH)
        for name, a in (("k", keys), ("v", values), ("q", queries), ("g", grad_out))
    }
    place = lax.axis_index("g").astype(jnp.int32).reshape(1)
    one, two = CHUNKS
    rows_one = to_tiles(tensors, [(name, 0, one) for name in "kvqg"])
    rows_two = to_tiles(tensors, [(name, one, two) for name in "kvqg"])

    kv_one, qg_one = edges(rows_one)
    kv_one, qg_one = to_plane(kv_one, 1), to_plane(qg_one, -1)
    dk, dv, stats, *dq = own_pass(place, rows_one, kv_one, one, 60)
    dq_one = to_slabs(dq)
    stats = to_plane(stats, -1)
    rows_two, stats = tied(rows_two, stats)
    dkv_one = to_slabs(later_pass(place, rows_one, qg_one, stats, dk, dv, one, 60))

    kv_two, qg_two = edges(rows_two)
    kv_two, qg_two = to_plane(kv_two, 1), to_plane(qg_two, -1)
    kv_two, dkv_one[0], *dq_one = tied(kv_two, dkv_one[0], *dq_one)
    dk, dv, stats, *dq = own_pass(place, rows_two, kv_two, two, 20)
    dq_two = to_slabs(dq)
    stats = to_plane(stats, -1)
    dkv = later_pass(place, rows_two, qg_two, stats, dk, dv, two, 20)
    early = tied(*dkv, *dkv_one, *dq_two)
    dkv, dkv_one, dq_two = early[:GROUP], early[GROUP : 2 * GROUP], early[2 * GROUP :]
    dkv_two = to_slabs(dkv)
    outs = unpack(place, [*dq_one, *dkv_one, *dq_two, *dkv_two])
    return tuple(out.reshape(FRAMES, SPOTS, HEADS * DH) for out in outs)


def solution(mesh):
    parted = Mesh(mesh.devices.reshape(PLANES, GROUP, FRAMES), ("z", "g", "tile"))
    given = P(("z", "g", "tile"), None, None)
    wanted = P(("z", "g"), "tile", None)
    return jax.shard_map(
        shards, mesh=parted, in_specs=(given,) * 4, out_specs=(wanted,) * 3, check_vma=False
    )
```

```python
import math

import jax
import jax.numpy as jnp
from jax import lax
from jax.experimental import pallas as pl
from jax.experimental.pallas import tpu as pltpu
from jax.sharding import Mesh, PartitionSpec as P

DH = 128
HEADS = 24
FRAMES = 8
SPOTS = 24
GROUP = 4
PLANES = 8
ROWS = FRAMES * SPOTS
OWN = GROUP * ROWS
HALO = 3 * ROWS
MINE = HEADS // GROUP
CHUNKS = (3, 3)
SCALE = 1.0 / math.sqrt(DH)
SCALE2 = SCALE * math.log2(math.e)
BF16 = jnp.bfloat16
F32 = jnp.float32
ANY = pl.BlockSpec(memory_space=pl.ANY)
PLACE = pl.BlockSpec(memory_space=pltpu.SMEM)


def nt(a, b):
    return lax.dot_general(a, b, (((1,), (1,)), ((), ())), preferred_element_type=F32)


def nn(a, b):
    return lax.dot_general(a, b, (((1,), (0,)), ((), ())), preferred_element_type=F32)


def tn(a, b):
    return lax.dot_general(a, b, (((0,), (0,)), ((), ())), preferred_element_type=F32)


def pack_kernel(parts, *refs):
    sources, (packed, held, sems) = refs[: len(parts)], refs[len(parts) :]
    loads, stores = [], []
    column = 0
    for index, (source, (_, first, heads)) in enumerate(zip(sources, parts)):
        width = heads * DH
        for group in range(GROUP):
            place = index * GROUP + group
            start = (group * MINE + first) * DH
            slot = held.at[place, :, :, pl.ds(0, width)]
            loads.append(
                pltpu.make_async_copy(
                    source.at[:, :, pl.ds(start, width)], slot, sems.at[0, place]
                )
            )
            stores.append(
                pltpu.make_async_copy(
                    slot, packed.at[group, :, :, pl.ds(column, width)], sems.at[1, place]
                )
            )
        column += width
    for load in loads:
        load.start()
    for load, store in zip(loads, stores):
        load.wait()
        store.start()
    for store in stores:
        store.wait()


def pack(tensors, parts):
    def body(*refs):
        pack_kernel(parts, *refs)

    count = len(parts) * GROUP
    most = max(heads for _, _, heads in parts)
    total = sum(heads for _, _, heads in parts)
    packed = pl.pallas_call(
        body,
        out_shape=jax.ShapeDtypeStruct((GROUP, FRAMES, SPOTS, total * DH), BF16),
        in_specs=[ANY] * len(parts),
        out_specs=ANY,
        scratch_shapes=[
            pltpu.VMEM((count, FRAMES, SPOTS, most * DH), BF16),
            pltpu.SemaphoreType.DMA((2, count)),
        ],
        compiler_params=pltpu.CompilerParams(vmem_limit_bytes=60 << 20),
        name="pack",
    )(*[tensors[name] for name, _, _ in parts])
    return packed.reshape(GROUP * FRAMES, SPOTS, total * DH)


def partner_of(place, partner):
    return lax.bitwise_xor(place, jnp.int32(partner))


def partner_rows(place, partner):
    return pl.ds(pl.multiple_of(partner_of(place[0], partner) * ROWS, ROWS), ROWS)


def slab_rows(first, count=1):
    return slice(first * ROWS, (first + count) * ROWS)


def own_kernel(place, q, k, v, g, hk, hv, *refs):
    (dk, dv, stats), dq_to, (dq, kx, vx) = refs[:3], refs[3:7], refs[7:]
    kx[:HALO] = hk[...]
    kx[HALO:] = k[...]
    vx[:HALO] = hv[...]
    vx[HALO:] = v[...]
    fronts = []
    for slab in range(GROUP):
        here, seen = slab_rows(slab), slab_rows(slab, 4)
        fronts.append((nt(kx[seen], q[here]), nt(vx[seen], g[here])))
    for slab, (scores, dprobs) in enumerate(fronts):
        here, seen, past = slab_rows(slab), slab_rows(slab, 4), slab * ROWS
        peak = jnp.max(scores, axis=0, keepdims=True) * SCALE2
        weights = jnp.exp2(scores * SCALE2 - peak)
        total = jnp.sum(weights, axis=0, keepdims=True)
        probs = weights * (1.0 / total)
        delta = jnp.sum(probs * dprobs, axis=0, keepdims=True)
        dscores = (probs * (dprobs - delta)).astype(BF16)
        low = probs.astype(BF16)
        stats[0, 2 * slab : 2 * slab + 1] = peak + jnp.log2(total)
        stats[0, 2 * slab + 1 : 2 * slab + 2] = delta
        dq[here] = (tn(kx[seen], dscores).T * SCALE).astype(BF16)
        part_k = nn(dscores[HALO - past :], q[here])
        part_v = nn(low[HALO - past :], g[here])
        if slab:
            dk[0, :past] += part_k[:past]
            dv[0, :past] += part_v[:past]
        dk[0, here] = part_k[past:]
        dv[0, here] = part_v[past:]
    for partner, target in enumerate(dq_to):
        target[...] = dq[partner_rows(place, partner)]


def own_pass(place, rows, halo, heads, room, work=1000):
    def col(start, rows=OWN):
        return pl.BlockSpec((rows, DH), lambda h: (0, start + h))

    part = pl.BlockSpec((1, OWN, DH), lambda h: (h, 0, 0))
    return pl.pallas_call(
        own_kernel,
        grid=(heads,),
        in_specs=[
            PLACE,
            col(2 * heads),
            col(0),
            col(heads),
            col(3 * heads),
            col(0, HALO),
            col(heads, HALO),
        ],
        out_specs=[part, part, pl.BlockSpec((1, 8, ROWS), lambda h: (h, 0, 0))]
        + [col(0, ROWS)] * GROUP,
        out_shape=[
            jax.ShapeDtypeStruct((heads, OWN, DH), F32),
            jax.ShapeDtypeStruct((heads, OWN, DH), F32),
            jax.ShapeDtypeStruct((heads, 8, ROWS), F32),
        ]
        + [jax.ShapeDtypeStruct((ROWS, heads * DH), BF16)] * GROUP,
        scratch_shapes=[pltpu.VMEM((OWN, DH), BF16)]
        + [pltpu.VMEM((OWN + HALO, DH), BF16)] * 2,
        compiler_params=pltpu.CompilerParams(vmem_limit_bytes=room << 20),
        cost_estimate=pl.CostEstimate(
            flops=work,
            bytes_accessed=1000,
            transcendentals=0,
        ),
        name="own_pass",
    )(place, rows, rows, rows, rows, halo, halo)


def later_kernel(place, k, v, hq, hg, stats, dk, dv, *refs):
    outs, (sk, sv) = refs[:GROUP], refs[GROUP:]
    sk[...] = dk[0]
    sv[...] = dv[0]
    fronts = []
    for slab in range(3):
        there, rest = slab_rows(slab), slice((slab + 1) * ROWS, OWN)
        fronts.append((nt(k[rest], hq[there]), nt(v[rest], hg[there])))
    for slab, (scores, dprobs) in enumerate(fronts):
        there, rest = slab_rows(slab), slice((slab + 1) * ROWS, OWN)
        lse = stats[0, 2 * slab : 2 * slab + 1]
        delta = stats[0, 2 * slab + 1 : 2 * slab + 2]
        probs = jnp.exp2(scores * SCALE2 - lse)
        dscores = (probs * (dprobs - delta)).astype(BF16)
        sk[rest] += nn(dscores, hq[there])
        sv[rest] += nn(probs.astype(BF16), hg[there])
    for partner, target in enumerate(outs):
        here = partner_rows(place, partner)
        target[0] = (sk[here] * SCALE).astype(BF16)
        target[1] = sv[here].astype(BF16)


def later_pass(place, rows, halo, stats, dk, dv, heads, room):
    def col(start, rows=OWN):
        return pl.BlockSpec((rows, DH), lambda h: (0, start + h))

    part = pl.BlockSpec((1, OWN, DH), lambda h: (h, 0, 0))
    return pl.pallas_call(
        later_kernel,
        grid=(heads,),
        in_specs=[
            PLACE,
            col(0),
            col(heads),
            col(0, HALO),
            col(heads, HALO),
            pl.BlockSpec((1, 8, ROWS), lambda h: (h, 0, 0)),
            part,
            part,
        ],
        out_specs=[pl.BlockSpec((2, ROWS, DH), lambda h: (0, 0, h))] * GROUP,
        out_shape=[jax.ShapeDtypeStruct((2, ROWS, heads * DH), BF16)] * GROUP,
        scratch_shapes=[pltpu.VMEM((OWN, DH), F32)] * 2,
        compiler_params=pltpu.CompilerParams(vmem_limit_bytes=room << 20),
        cost_estimate=pl.CostEstimate(
            flops=1000,
            bytes_accessed=1000,
            transcendentals=0,
        ),
        name="later_pass",
    )(place, rows, rows, halo, halo, stats, dk, dv)


def unpack_kernel(place, *refs):
    count = 2 * len(CHUNKS) * GROUP
    pieces, outs, (held, load_sems, store_sems) = refs[:count], refs[count : count + 3], refs[count + 3 :]
    loads = [[], [], []]
    first = 0
    for chunk, heads in enumerate(CHUNKS):
        for partner in range(GROUP):
            column = (partner_of(place[0], partner) * MINE + first) * DH
            columns = pl.ds(pl.multiple_of(column, DH), heads * DH)
            dq = pieces[2 * chunk * GROUP + partner]
            dkv = pieces[(2 * chunk + 1) * GROUP + partner]
            for index, source in enumerate((dq, dkv.at[0], dkv.at[1])):
                loads[index].append(
                    pltpu.make_async_copy(
                        source,
                        held.at[index, :, columns],
                        load_sems.at[index, chunk * GROUP + partner],
                    )
                )
        first += heads
    for load in loads[0] + loads[1] + loads[2]:
        load.start()
    stores = []
    for index in range(3):
        for load in loads[index]:
            load.wait()
        stores.append(pltpu.make_async_copy(held.at[index], outs[index], store_sems.at[index]))
        stores[-1].start()
    for store in stores:
        store.wait()


def unpack(place, pieces):
    shape = jax.ShapeDtypeStruct((ROWS, HEADS * DH), BF16)
    return pl.pallas_call(
        unpack_kernel,
        out_shape=[shape] * 3,
        in_specs=[PLACE] + [ANY] * len(pieces),
        out_specs=[ANY] * 3,
        scratch_shapes=[
            pltpu.VMEM((3, ROWS, HEADS * DH), BF16),
            pltpu.SemaphoreType.DMA((3, len(CHUNKS) * GROUP)),
            pltpu.SemaphoreType.DMA((3,)),
        ],
        compiler_params=pltpu.CompilerParams(vmem_limit_bytes=8 << 20),
        name="unpack",
    )(place, *pieces)


def edges_kernel(rows, kv, qg, held_kv, held_qg, sems):
    width = kv.shape[1]
    loads = (
        pltpu.make_async_copy(rows.at[pl.ds(ROWS, HALO), pl.ds(0, width)], held_kv, sems.at[0]),
        pltpu.make_async_copy(rows.at[pl.ds(0, HALO), pl.ds(width, width)], held_qg, sems.at[1]),
    )
    stores = (
        pltpu.make_async_copy(held_kv, kv, sems.at[2]),
        pltpu.make_async_copy(held_qg, qg, sems.at[3]),
    )
    for load in loads:
        load.start()
    for load, store in zip(loads, stores):
        load.wait()
        store.start()
    for store in stores:
        store.wait()


def edges(rows):
    width = rows.shape[1] // 2
    return pl.pallas_call(
        edges_kernel,
        out_shape=[jax.ShapeDtypeStruct((HALO, width), BF16)] * 2,
        in_specs=[ANY],
        out_specs=[ANY] * 2,
        scratch_shapes=[pltpu.VMEM((HALO, width), BF16)] * 2 + [pltpu.SemaphoreType.DMA((4,))],
        compiler_params=pltpu.CompilerParams(vmem_limit_bytes=4 << 20),
        name="edges",
    )(rows)


def to_plane(block, step):
    return lax.ppermute(block, "z", [(i, (i + step) % PLANES) for i in range(PLANES)])


def to_tiles(packed):
    return lax.all_to_all(packed, ("g", "tile"), 0, 0, tiled=True).reshape(OWN, -1)


def to_slabs(blocks):
    sent = [
        lax.ppermute(block, "g", [(i, i ^ partner) for i in range(GROUP)])
        for partner, block in enumerate(blocks)
        if partner
    ]
    return [blocks[0], *sent]


def tied(*arrays):
    return lax.optimization_barrier(arrays)


def shards(queries, keys, values, grad_out):
    tensors = {
        name: a.reshape(FRAMES, SPOTS, HEADS * DH)
        for name, a in (("k", keys), ("v", values), ("q", queries), ("g", grad_out))
    }
    place = lax.axis_index("g").astype(jnp.int32).reshape(1)
    one, two = CHUNKS
    rows_one = to_tiles(pack(tensors, [(name, 0, one) for name in "kvqg"]))
    packed_two = pack(tensors, [(name, one, two) for name in "kvqg"])
    rows_one, packed_two = tied(rows_one, packed_two)
    rows_two = to_tiles(packed_two)

    kv_one, qg_one = edges(rows_one)
    kv_one, qg_one = to_plane(kv_one, 1), to_plane(qg_one, -1)
    dk, dv, stats, *dq = own_pass(place, rows_one, kv_one, one, 60, 200_000_000_000)
    dq_one = to_slabs(dq)
    stats = to_plane(stats, -1)
    rows_two, stats = tied(rows_two, stats)
    dkv_one = to_slabs(later_pass(place, rows_one, qg_one, stats, dk, dv, one, 60))

    kv_two, qg_two = edges(rows_two)
    kv_two, qg_two = to_plane(kv_two, 1), to_plane(qg_two, -1)
    kv_two, dkv_one[0], *dq_one = tied(kv_two, dkv_one[0], *dq_one)
    dk, dv, stats, *dq = own_pass(place, rows_two, kv_two, two, 20)
    dq_two = to_slabs(dq)
    stats = to_plane(stats, -1)
    dkv = later_pass(place, rows_two, qg_two, stats, dk, dv, two, 20)
    early = tied(*dkv, *dkv_one, *dq_two)
    dkv, dkv_one, dq_two = early[:GROUP], early[GROUP : 2 * GROUP], early[2 * GROUP :]
    dkv_two = to_slabs(dkv)
    outs = unpack(place, [*dq_one, *dkv_one, *dq_two, *dkv_two])
    return tuple(out.reshape(FRAMES, SPOTS, HEADS * DH) for out in outs)


def solution(mesh):
    parted = Mesh(mesh.devices.reshape(PLANES, GROUP, FRAMES), ("z", "g", "tile"))
    given = P(("z", "g", "tile"), None, None)
    wanted = P(("z", "g"), "tile", None)
    return jax.shard_map(
        shards, mesh=parted, in_specs=(given,) * 4, out_specs=(wanted,) * 3, check_vma=False
    )
```

```python
import math

import jax
import jax.numpy as jnp
from jax import lax
from jax.experimental import pallas as pl
from jax.experimental.pallas import tpu as pltpu
from jax.sharding import Mesh, PartitionSpec as P

DH = 128
HEADS = 24
FRAMES = 8
SPOTS = 24
GROUP = 4
PLANES = 8
ROWS = FRAMES * SPOTS
OWN = GROUP * ROWS
HALO = 3 * ROWS
MINE = HEADS // GROUP
CHUNKS = (3, 3)
SCALE = 1.0 / math.sqrt(DH)
SCALE2 = SCALE * math.log2(math.e)
BF16 = jnp.bfloat16
F32 = jnp.float32
ANY = pl.BlockSpec(memory_space=pl.ANY)
PLACE = pl.BlockSpec(memory_space=pltpu.SMEM)


def nt(a, b):
    return lax.dot_general(a, b, (((1,), (1,)), ((), ())), preferred_element_type=F32)


def nn(a, b):
    return lax.dot_general(a, b, (((1,), (0,)), ((), ())), preferred_element_type=F32)


def tn(a, b):
    return lax.dot_general(a, b, (((0,), (0,)), ((), ())), preferred_element_type=F32)


def pack_kernel(parts, *refs):
    sources, (packed, held, sems) = refs[: len(parts)], refs[len(parts) :]
    loads, stores = [], []
    column = 0
    for index, (source, (_, first, heads)) in enumerate(zip(sources, parts)):
        width = heads * DH
        for group in range(GROUP):
            place = index * GROUP + group
            start = (group * MINE + first) * DH
            slot = held.at[place, :, :, pl.ds(0, width)]
            loads.append(
                pltpu.make_async_copy(
                    source.at[:, :, pl.ds(start, width)], slot, sems.at[0, place]
                )
            )
            stores.append(
                pltpu.make_async_copy(
                    slot, packed.at[group, :, :, pl.ds(column, width)], sems.at[1, place]
                )
            )
        column += width
    for load in loads:
        load.start()
    for load, store in zip(loads, stores):
        load.wait()
        store.start()
    for store in stores:
        store.wait()


def pack(tensors, parts):
    def body(*refs):
        pack_kernel(parts, *refs)

    count = len(parts) * GROUP
    most = max(heads for _, _, heads in parts)
    total = sum(heads for _, _, heads in parts)
    packed = pl.pallas_call(
        body,
        out_shape=jax.ShapeDtypeStruct((GROUP, FRAMES, SPOTS, total * DH), BF16),
        in_specs=[ANY] * len(parts),
        out_specs=ANY,
        scratch_shapes=[
            pltpu.VMEM((count, FRAMES, SPOTS, most * DH), BF16),
            pltpu.SemaphoreType.DMA((2, count)),
        ],
        compiler_params=pltpu.CompilerParams(vmem_limit_bytes=60 << 20),
        name="pack",
    )(*[tensors[name] for name, _, _ in parts])
    return packed.reshape(GROUP * FRAMES, SPOTS, total * DH)


def partner_of(place, partner):
    return lax.bitwise_xor(place, jnp.int32(partner))


def partner_rows(place, partner):
    return pl.ds(pl.multiple_of(partner_of(place[0], partner) * ROWS, ROWS), ROWS)


def slab_rows(first, count=1):
    return slice(first * ROWS, (first + count) * ROWS)


def own_kernel(place, q, k, v, g, hk, hv, *refs):
    (dk, dv, stats), dq_to, (dq, kx, vx) = refs[:3], refs[3:7], refs[7:]
    kx[:HALO] = hk[...]
    kx[HALO:] = k[...]
    vx[:HALO] = hv[...]
    vx[HALO:] = v[...]
    fronts = []
    for slab in range(GROUP):
        here, seen = slab_rows(slab), slab_rows(slab, 4)
        fronts.append((nt(kx[seen], q[here]), nt(vx[seen], g[here])))
    for slab, (scores, dprobs) in enumerate(fronts):
        here, seen, past = slab_rows(slab), slab_rows(slab, 4), slab * ROWS
        peak = jnp.max(scores, axis=0, keepdims=True) * SCALE2
        weights = jnp.exp2(scores * SCALE2 - peak)
        total = jnp.sum(weights, axis=0, keepdims=True)
        probs = weights * (1.0 / total)
        delta = jnp.sum(probs * dprobs, axis=0, keepdims=True)
        dscores = (probs * (dprobs - delta)).astype(BF16)
        low = probs.astype(BF16)
        stats[0, 2 * slab : 2 * slab + 1] = peak + jnp.log2(total)
        stats[0, 2 * slab + 1 : 2 * slab + 2] = delta
        dq[here] = (tn(kx[seen], dscores).T * SCALE).astype(BF16)
        part_k = nn(dscores[HALO - past :], q[here])
        part_v = nn(low[HALO - past :], g[here])
        if slab:
            dk[0, :past] += part_k[:past]
            dv[0, :past] += part_v[:past]
        dk[0, here] = part_k[past:]
        dv[0, here] = part_v[past:]
    for partner, target in enumerate(dq_to):
        target[...] = dq[partner_rows(place, partner)]


def own_pass(place, rows, halo, heads, room, work=1000):
    def col(start, rows=OWN):
        return pl.BlockSpec((rows, DH), lambda h: (0, start + h))

    part = pl.BlockSpec((1, OWN, DH), lambda h: (h, 0, 0))
    return pl.pallas_call(
        own_kernel,
        grid=(heads,),
        in_specs=[
            PLACE,
            col(2 * heads),
            col(0),
            col(heads),
            col(3 * heads),
            col(0, HALO),
            col(heads, HALO),
        ],
        out_specs=[part, part, pl.BlockSpec((1, 8, ROWS), lambda h: (h, 0, 0))]
        + [col(0, ROWS)] * GROUP,
        out_shape=[
            jax.ShapeDtypeStruct((heads, OWN, DH), F32),
            jax.ShapeDtypeStruct((heads, OWN, DH), F32),
            jax.ShapeDtypeStruct((heads, 8, ROWS), F32),
        ]
        + [jax.ShapeDtypeStruct((ROWS, heads * DH), BF16)] * GROUP,
        scratch_shapes=[pltpu.VMEM((OWN, DH), BF16)]
        + [pltpu.VMEM((OWN + HALO, DH), BF16)] * 2,
        compiler_params=pltpu.CompilerParams(vmem_limit_bytes=room << 20),
        cost_estimate=pl.CostEstimate(
            flops=work,
            bytes_accessed=1000,
            transcendentals=0,
        ),
        name="own_pass",
    )(place, rows, rows, rows, rows, halo, halo)


def later_kernel(place, k, v, hq, hg, stats, dk, dv, *refs):
    outs, (sk, sv) = refs[:GROUP], refs[GROUP:]
    sk[...] = dk[0]
    sv[...] = dv[0]
    fronts = []
    for slab in range(3):
        there, rest = slab_rows(slab), slice((slab + 1) * ROWS, OWN)
        fronts.append((nt(k[rest], hq[there]), nt(v[rest], hg[there])))
    for slab, (scores, dprobs) in enumerate(fronts):
        there, rest = slab_rows(slab), slice((slab + 1) * ROWS, OWN)
        lse = stats[0, 2 * slab : 2 * slab + 1]
        delta = stats[0, 2 * slab + 1 : 2 * slab + 2]
        probs = jnp.exp2(scores * SCALE2 - lse)
        dscores = (probs * (dprobs - delta)).astype(BF16)
        sk[rest] += nn(dscores, hq[there])
        sv[rest] += nn(probs.astype(BF16), hg[there])
    for partner, target in enumerate(outs):
        here = partner_rows(place, partner)
        target[0] = (sk[here] * SCALE).astype(BF16)
        target[1] = sv[here].astype(BF16)


def later_pass(place, rows, halo, stats, dk, dv, heads, room):
    def col(start, rows=OWN):
        return pl.BlockSpec((rows, DH), lambda h: (0, start + h))

    part = pl.BlockSpec((1, OWN, DH), lambda h: (h, 0, 0))
    return pl.pallas_call(
        later_kernel,
        grid=(heads,),
        in_specs=[
            PLACE,
            col(0),
            col(heads),
            col(0, HALO),
            col(heads, HALO),
            pl.BlockSpec((1, 8, ROWS), lambda h: (h, 0, 0)),
            part,
            part,
        ],
        out_specs=[pl.BlockSpec((2, ROWS, DH), lambda h: (0, 0, h))] * GROUP,
        out_shape=[jax.ShapeDtypeStruct((2, ROWS, heads * DH), BF16)] * GROUP,
        scratch_shapes=[pltpu.VMEM((OWN, DH), F32)] * 2,
        compiler_params=pltpu.CompilerParams(vmem_limit_bytes=room << 20),
        cost_estimate=pl.CostEstimate(
            flops=1000,
            bytes_accessed=1000,
            transcendentals=0,
        ),
        name="later_pass",
    )(place, rows, rows, halo, halo, stats, dk, dv)


def unpack_kernel(place, *refs):
    count = 2 * len(CHUNKS) * GROUP
    pieces, outs, (held, load_sems, store_sems) = refs[:count], refs[count : count + 3], refs[count + 3 :]
    loads = [[], [], []]
    first = 0
    for chunk, heads in enumerate(CHUNKS):
        for partner in range(GROUP):
            column = (partner_of(place[0], partner) * MINE + first) * DH
            columns = pl.ds(pl.multiple_of(column, DH), heads * DH)
            dq = pieces[2 * chunk * GROUP + partner]
            dkv = pieces[(2 * chunk + 1) * GROUP + partner]
            for index, source in enumerate((dq, dkv.at[0], dkv.at[1])):
                loads[index].append(
                    pltpu.make_async_copy(
                        source,
                        held.at[index, :, columns],
                        load_sems.at[index, chunk * GROUP + partner],
                    )
                )
        first += heads
    for load in loads[0] + loads[1] + loads[2]:
        load.start()
    stores = []
    for index in range(3):
        for load in loads[index]:
            load.wait()
        stores.append(pltpu.make_async_copy(held.at[index], outs[index], store_sems.at[index]))
        stores[-1].start()
    for store in stores:
        store.wait()


def unpack(place, pieces):
    shape = jax.ShapeDtypeStruct((ROWS, HEADS * DH), BF16)
    return pl.pallas_call(
        unpack_kernel,
        out_shape=[shape] * 3,
        in_specs=[PLACE] + [ANY] * len(pieces),
        out_specs=[ANY] * 3,
        scratch_shapes=[
            pltpu.VMEM((3, ROWS, HEADS * DH), BF16),
            pltpu.SemaphoreType.DMA((3, len(CHUNKS) * GROUP)),
            pltpu.SemaphoreType.DMA((3,)),
        ],
        compiler_params=pltpu.CompilerParams(vmem_limit_bytes=8 << 20),
        name="unpack",
    )(place, *pieces)


def edges_kernel(rows, kv, qg, held_kv, held_qg, sems):
    width = kv.shape[1]
    loads = (
        pltpu.make_async_copy(rows.at[pl.ds(ROWS, HALO), pl.ds(0, width)], held_kv, sems.at[0]),
        pltpu.make_async_copy(rows.at[pl.ds(0, HALO), pl.ds(width, width)], held_qg, sems.at[1]),
    )
    stores = (
        pltpu.make_async_copy(held_kv, kv, sems.at[2]),
        pltpu.make_async_copy(held_qg, qg, sems.at[3]),
    )
    for load in loads:
        load.start()
    for load, store in zip(loads, stores):
        load.wait()
        store.start()
    for store in stores:
        store.wait()


def edges(rows):
    width = rows.shape[1] // 2
    return pl.pallas_call(
        edges_kernel,
        out_shape=[jax.ShapeDtypeStruct((HALO, width), BF16)] * 2,
        in_specs=[ANY],
        out_specs=[ANY] * 2,
        scratch_shapes=[pltpu.VMEM((HALO, width), BF16)] * 2 + [pltpu.SemaphoreType.DMA((4,))],
        compiler_params=pltpu.CompilerParams(vmem_limit_bytes=4 << 20),
        name="edges",
    )(rows)


def to_plane(block, step):
    return lax.ppermute(block, "z", [(i, (i + step) % PLANES) for i in range(PLANES)])


def to_tiles(packed):
    return lax.all_to_all(packed, ("g", "tile"), 0, 0, tiled=True).reshape(OWN, -1)


def to_slabs(blocks):
    sent = [
        lax.ppermute(block, "g", [(i, i ^ partner) for i in range(GROUP)])
        for partner, block in enumerate(blocks)
        if partner
    ]
    return [blocks[0], *sent]


def tied(*arrays):
    return lax.optimization_barrier(arrays)


def shards(queries, keys, values, grad_out):
    tensors = {
        name: a.reshape(FRAMES, SPOTS, HEADS * DH)
        for name, a in (("k", keys), ("v", values), ("q", queries), ("g", grad_out))
    }
    place = lax.axis_index("g").astype(jnp.int32).reshape(1)
    one, two = CHUNKS
    rows_one = to_tiles(pack(tensors, [(name, 0, one) for name in "kvqg"]))
    packed_two = pack(tensors, [(name, one, two) for name in "kvqg"])
    rows_one, packed_two = tied(rows_one, packed_two)
    rows_two = to_tiles(packed_two)

    kv_one, qg_one = edges(rows_one)
    kv_one, qg_one = to_plane(kv_one, 1), to_plane(qg_one, -1)
    dk, dv, stats, *dq = own_pass(place, rows_one, kv_one, one, 59, 200_000_000_000)
    dq_one = to_slabs(dq)
    stats = to_plane(stats, -1)
    rows_two, stats = tied(rows_two, stats)
    dkv_one = to_slabs(later_pass(place, rows_one, qg_one, stats, dk, dv, one, 60))

    kv_two, qg_two = edges(rows_two)
    kv_two, qg_two = to_plane(kv_two, 1), to_plane(qg_two, -1)
    kv_two, dkv_one[0], *dq_one = tied(kv_two, dkv_one[0], *dq_one)
    dk, dv, stats, *dq = own_pass(place, rows_two, kv_two, two, 20)
    dq_two = to_slabs(dq)
    stats = to_plane(stats, -1)
    dkv = later_pass(place, rows_two, qg_two, stats, dk, dv, two, 20)
    early = tied(*dkv, *dkv_one, *dq_two)
    dkv, dkv_one, dq_two = early[:GROUP], early[GROUP : 2 * GROUP], early[2 * GROUP :]
    dkv_two = to_slabs(dkv)
    outs = unpack(place, [*dq_one, *dkv_one, *dq_two, *dkv_two])
    return tuple(out.reshape(FRAMES, SPOTS, HEADS * DH) for out in outs)


def solution(mesh):
    parted = Mesh(mesh.devices.reshape(PLANES, GROUP, FRAMES), ("z", "g", "tile"))
    given = P(("z", "g", "tile"), None, None)
    wanted = P(("z", "g"), "tile", None)
    return jax.shard_map(
        shards, mesh=parted, in_specs=(given,) * 4, out_specs=(wanted,) * 3, check_vma=False
    )
```
